256 devices in a mesh: seq: 64 (over z, x, core), chan: 4 (over y).
Axes of the slice: x: 4, y: 4, z: 8, core: 2. Of those that a mesh axis runs over, the one named last changes fastest.
Arguments:
- tokens: bfloat16 [24576, 4096], P('seq'), as said below
- norm_gain: float32 [4096], replicated, may hold values from 0.1 to 1.9
- in_weight: bfloat16 [4096, 3, 4096], P('seq', None, 'chan'), may hold values from -0.09375 to 0.09375
- short_taps: float32 [3, 7, 4096], P(None, None, 'chan'), may hold values from -2 to 2
- decay_rates: float32 [16, 4096], P(None, 'chan'), as said below
- residues: float32 [16, 4096], P(None, 'chan'), may hold values from -3 to 3
- bypass: float32 [4096], P('chan'), may hold values from -4 to 4
- out_weight: bfloat16 [4096, 4096], P('chan'), may hold values from -0.09375 to 0.09375
Outputs:
- block_out: bfloat16 [24576, 4096], P('seq', 'chan')
The draws below stay inside these ranges and needn't reach their ends.
Inputs may be any that keep to these rules, and one draw needn't show every extreme that they name: `tokens`: residual stream activations. `decay_rates`: positive decay rates of the modes.
All inputs are finite; a program needn't handle non-finite values.
Results may differ from the reference program's by a relative error of at most 0.029.
Values may be sent and summed in bfloat16 or wider, within the bound.
No kernel may reach another device: no remote copies, remote signals or barrier semaphores. Data moves between devices by JAX's collectives and lax.ppermute only.
A program may use at most 256 MiB of HBM per device.

```python
import math
import jax
import jax.numpy as jnp
from jax import lax

DW = 4096
C = 4096
MODES = 16
SHORT = 7
BLOCK = 64
TOKENS = 24576
C_DEV = 1024
N_CHAN = 4


def draw_tokens(key, part):
    key = jax.random.fold_in(key, 11)
    first, second, third = jax.random.split(key, 3)
    column_scale = jnp.exp(jax.random.uniform(third, (1, DW), jnp.float32, 0.0, math.log(10.0)))
    base = jnp.clip(jax.random.normal(first, (TOKENS, DW), jnp.float32), -6.0, 6.0)
    row_scale = jnp.exp(jax.random.uniform(second, (TOKENS, 1), jnp.float32, 0.0, math.log(10.0)))
    values = base * row_scale * column_scale
    return values.astype(jnp.bfloat16)


def draw_decay_rates(key, part):
    key = jax.random.fold_in(key, 23)
    first, second, third = jax.random.split(key, 3)
    slow_share = 0.5
    slow_low = 0.3
    slow_high = 2.3
    is_slow = jax.random.uniform(first, (MODES, C), jnp.float32) < slow_share
    slow_rate = jnp.exp(jax.random.uniform(second, (MODES, C), jnp.float32, math.log(slow_low), math.log(slow_high))) / TOKENS
    fast_rate = jnp.exp(jax.random.uniform(third, (MODES, C), jnp.float32, math.log(1.0 / 50.0), math.log(1.0 / 30.0)))
    return jnp.where(is_slow, slow_rate, fast_rate).astype(jnp.float32)


def block_levels(stream_key, extent, pieces, low, high):
    level = 1.0
    for axis_at, parts in pieces:
        draws = jax.random.uniform(jax.random.fold_in(jax.random.fold_in(stream_key, 6), axis_at), (parts,), jnp.float32, low / len(pieces), high / len(pieces))
        level = level * jnp.repeat(jnp.exp(draws), extent[axis_at] // parts).reshape((-1,) + (1,) * (len(extent) - 1 - axis_at))
    return level


def bell_draw(stream_key, extent, spread, limit, cuts=(), held_as=jnp.bfloat16):
    array = spread * jax.random.normal(stream_key, extent, jnp.float32)
    if cuts:
        array = array * block_levels(stream_key, extent, cuts, -0.22, 0.18)
    return jnp.clip(array, -limit, limit).astype(held_as)


def setup_inputs(seed: int = 0) -> dict:
    key_of = jax.random.split(jax.random.key(seed), 9)
    return {
        "tokens": draw_tokens(jax.random.fold_in(key_of[8], 71), 0),
        "norm_gain": jnp.clip(1.0 + 0.18 * jax.random.normal(key_of[1], (DW,), jnp.float32), 0.1, 1.9),
        "in_weight": bell_draw(key_of[2], (DW, 3, C), DW ** -0.5, 0.09375, ((0, 64), (2, 4))),
        "short_taps": bell_draw(key_of[3], (3, SHORT, C), SHORT ** -0.5, 2.0, ((2, 4),), jnp.float32),
        "decay_rates": draw_decay_rates(jax.random.fold_in(key_of[8], 71), 0),
        "residues": bell_draw(key_of[5], (MODES, C), 0.5, 3.0, ((1, 4),), jnp.float32),
        "bypass": bell_draw(key_of[6], (C,), 1.0, 4.0, ((0, 4),), jnp.float32),
        "out_weight": bell_draw(key_of[7], (C, DW), C ** -0.5, 0.09375, ((0, 4),)),
    }


def block_powers(decay_rates):
    lags = jnp.arange(BLOCK + 1).astype(jnp.float32)
    return jnp.exp(-decay_rates[None, :, :] * lags[:, None, None])

def reference(tokens, norm_gain, in_weight, short_taps, decay_rates, residues, bypass, out_weight):
    widened = tokens.astype(jnp.float32)
    square_mean = lax.optimization_barrier(jnp.mean(widened * widened, axis=1, keepdims=True))
    normed = (widened * lax.rsqrt(square_mean + 1e-05) * norm_gain.astype(jnp.float32)[None, :]).astype(jnp.bfloat16)
    projected = jnp.dot(normed, in_weight.reshape(DW, 3 * C), preferred_element_type=jnp.float32)
    projected = projected.astype(jnp.bfloat16).reshape(TOKENS, 3, C)
    padded = jnp.concatenate([jnp.zeros((SHORT - 1, 3, C), jnp.bfloat16), projected], axis=0).astype(jnp.float32)
    taps_wide = short_taps.astype(jnp.float32)
    featured = jnp.zeros((TOKENS, 3, C), jnp.float32)
    for offset in range(SHORT):
        featured = featured + taps_wide[None, :, offset, :] * padded[SHORT - 1 - offset:SHORT - 1 - offset + TOKENS]
    gated = (featured[:, 1, :] * featured[:, 2, :]).astype(jnp.bfloat16)
    powers = block_powers(decay_rates)
    mode_gain = residues * jnp.sqrt(-jnp.expm1(-2.0 * decay_rates))
    filter_taps = lax.optimization_barrier(jnp.sum(mode_gain[None, :, :] * powers[:BLOCK], axis=1))
    lag_rows = (jnp.arange(BLOCK)[:, None] - jnp.arange(BLOCK)[None, :]).astype(jnp.int32)
    toeplitz = jnp.where((lag_rows >= 0)[:, :, None], filter_taps[jnp.clip(lag_rows, 0, BLOCK - 1)], 0.0)
    entering = mode_gain[None, :, :] * powers[1:]
    leaving = jnp.flip(powers[:BLOCK], axis=0)
    decay_block = powers[BLOCK]
    gated_wide = gated.astype(jnp.float32)
    blocks = gated_wide.reshape(TOKENS // BLOCK, BLOCK, C)

    def advance(state, block_in):
        inside = jnp.einsum('tsc,sc->tc', toeplitz, block_in, precision=lax.Precision.HIGHEST)
        carried = jnp.einsum('tmc,mc->tc', entering, state, precision=lax.Precision.HIGHEST)
        added = jnp.einsum('smc,sc->mc', leaving, block_in, precision=lax.Precision.HIGHEST)
        return (decay_block * state + added, inside + carried)
    _, outputs = lax.scan(advance, jnp.zeros((MODES, C), jnp.float32), blocks)
    convolved = outputs.reshape(TOKENS, C)
    modulated = (featured[:, 0, :] * (convolved + bypass.astype(jnp.float32)[None, :] * gated_wide)).astype(jnp.bfloat16)
    block_out = jnp.zeros((TOKENS, DW), jnp.float32)
    for group in range(N_CHAN):
        partial_term = jnp.dot(modulated[:, group * C_DEV:(group + 1) * C_DEV], out_weight[group * C_DEV:(group + 1) * C_DEV], preferred_element_type=jnp.float32)
        block_out = block_out + lax.optimization_barrier(partial_term.astype(jnp.bfloat16)).astype(jnp.float32)
    return block_out.astype(jnp.bfloat16)
```

```python
import functools

import jax
import jax.numpy as jnp
from jax import lax
from jax.experimental import pallas as pl
from jax.experimental.pallas import tpu as pltpu
from jax.sharding import Mesh, PartitionSpec as P

SHORT = 7
MODES = 16
LANES = 128
UNIT = 128
HALO = 16
VMEM = 48 * 1024 * 1024
bf16, f32 = jnp.bfloat16, jnp.float32


def shift(block, axes, distance):
    count = lax.axis_size(axes)
    return lax.ppermute(block, axes, [(i, (i + distance) % count) for i in range(count)])


def from_behind(block, axes, distance):
    count = lax.axis_size(axes)
    return lax.ppermute(block, axes, [(i, i + distance) for i in range(count - distance)])


def params():
    return pltpu.CompilerParams(vmem_limit_bytes=VMEM)


def norm_kernel(core_ref, own_ref, other_ref, halo_ref, gain_ref, out_ref):
    gain = gain_ref[...]

    def put(rows, src):
        wide = src.astype(f32)
        mean = jnp.mean(wide * wide, axis=1, keepdims=True)
        out_ref[rows, :] = (wide * lax.rsqrt(mean + 1e-05) * gain).astype(bf16)

    put(pl.ds(0, HALO), halo_ref[...])
    count = own_ref.shape[0]
    step = 64

    def body(i, _):
        core = core_ref[0]
        at = pl.multiple_of(i * step, step)
        own_at = pl.multiple_of(HALO + core * count + i * step, HALO)
        other_at = pl.multiple_of(HALO + (1 - core) * count + i * step, HALO)
        put(pl.ds(own_at, step), own_ref[pl.ds(at, step), :])
        put(pl.ds(other_at, step), other_ref[pl.ds(at, step), :])
        return 0

    lax.fori_loop(0, count // step, body, 0)


def norm(core, own, other, halo, gain):
    rows, width = own.shape
    whole = pl.BlockSpec(memory_space=pltpu.VMEM)
    return pl.pallas_call(
        norm_kernel,
        out_shape=jax.ShapeDtypeStruct((HALO + 2 * rows, width), bf16),
        in_specs=[pl.BlockSpec(memory_space=pltpu.SMEM)] + [whole] * 4,
        out_specs=whole,
        compiler_params=params(),
        name="norm",
    )(core, own, other, halo, gain.reshape(1, width))


def project_kernel(counts, has_acc, offs_ref, *refs):
    total = sum(counts)
    cols, refs = refs[:total], refs[total:]
    pieces, refs = refs[: len(counts)], refs[len(counts) :]
    out_ref = refs[-1]
    left = jnp.concatenate([c[...] for c in cols], axis=1)
    right = jnp.concatenate(
        [p[...].reshape(n * UNIT, p.shape[-1]) for p, n in zip(pieces, counts)], axis=0
    )
    got = jnp.dot(left, right, preferred_element_type=f32)
    if has_acc:
        got = got + refs[0][0]
    out_ref[0] = got


def project(normed, acc, pieces, places):
    rows = normed.shape[0]
    streams, width = pieces[0].shape[1], pieces[0].shape[-1]
    counts = tuple(p.shape[0] for p in pieces)
    total = sum(counts)
    offs = jnp.stack([jnp.asarray(p, jnp.int32) for p in places])
    assert offs.shape == (total,)
    in_specs = [
        pl.BlockSpec((rows, UNIT), functools.partial(lambda u, j, offs: (0, offs[u]), u))
        for u in range(total)
    ]
    in_specs += [
        pl.BlockSpec((n, 1, UNIT, width), lambda j, offs: (0, j, 0, 0)) for n in counts
    ]
    args = [normed] * total + list(pieces)
    out_spec = pl.BlockSpec((1, rows, width), lambda j, offs: (j, 0, 0))
    aliases = {}
    if acc is not None:
        in_specs.append(out_spec)
        aliases = {1 + len(args): 0}
        args.append(acc)
    flops = 2 * rows * total * UNIT * streams * width
    return pl.pallas_call(
        functools.partial(project_kernel, counts, acc is not None),
        grid_spec=pltpu.PrefetchScalarGridSpec(
            num_scalar_prefetch=1, grid=(streams,), in_specs=in_specs, out_specs=out_spec
        ),
        out_shape=jax.ShapeDtypeStruct((streams, rows, width), f32),
        input_output_aliases=aliases,
        compiler_params=params(),
        cost_estimate=pl.CostEstimate(
            flops=flops, bytes_accessed=rows * streams * width * 8, transcendentals=0
        ),
        name="project",
    )(offs, *args)


def join_kernel(count, *refs):
    for u in range(count):
        refs[-1][u] = refs[u][0]


def join(pieces, after=()):
    whole = pl.BlockSpec(memory_space=pltpu.VMEM)
    return pl.pallas_call(
        functools.partial(join_kernel, len(pieces)),
        out_shape=jax.ShapeDtypeStruct((len(pieces),) + pieces[0].shape[1:], bf16),
        in_specs=[whole] * len(pieces) + [pl.BlockSpec(memory_space=pl.ANY)] * len(after),
        out_specs=whole,
        compiler_params=params(),
        name="join",
    )(*pieces, *after)


def project_all_kernel(core_ref, left_ref, right_ref, out_ref):
    out_ref[...] = jnp.dot(left_ref[...], right_ref[0], preferred_element_type=f32)


def project_all(core, normed, weight, width):
    rows, deep = normed.shape
    block = 256
    per_core = width // block
    return pl.pallas_call(
        project_all_kernel,
        grid_spec=pltpu.PrefetchScalarGridSpec(
            num_scalar_prefetch=1,
            grid=(per_core,),
            in_specs=[
                pl.BlockSpec((rows, deep), lambda j, core: (0, 0)),
                pl.BlockSpec((1, deep, block), lambda j, core: (0, 0, core[0] * per_core + j)),
            ],
            out_specs=pl.BlockSpec((rows, block), lambda j, core: (0, j)),
        ),
        out_shape=jax.ShapeDtypeStruct((rows, width), f32),
        compiler_params=params(),
        cost_estimate=pl.CostEstimate(
            flops=2 * rows * deep * width, bytes_accessed=rows * deep * 2, transcendentals=0
        ),
        name="project_all",
    )(core, normed, weight)


def spread(wide_ref, at, depth, half, tile, val):
    rows = pl.ds(at * 8 + half * 4 + tile, depth, stride=8)
    wide_ref[rows, :] = val.astype(bf16).astype(f32)


def convolve_short(wide_ref, taps_ref, j, base, step):
    reach = step + SHORT - 1
    rows = pl.ds(pl.multiple_of((base + HALO - (SHORT - 1)) * 8, 8), reach * 8)
    x = wide_ref[rows, :].reshape(reach, 8, LANES)
    total = taps_ref[j, 0][None] * x[SHORT - 1 : SHORT - 1 + step]
    for i in range(1, SHORT):
        total = total + taps_ref[j, i][None] * x[SHORT - 1 - i : SHORT - 1 - i + step]
    return total


def gate_kernel(rows, a_ref, b_ref, taps_ref, decay_ref, reach_ref, g_ref, e0_ref, e_ref, wide_ref):
    depth = rows + HALO
    for j in range(2):
        for half in range(2):
            for tile in range(4):
                src = (a_ref, b_ref)[tile // 2]
                col = (tile % 2) * LANES
                val = src[j, half * rows : half * rows + depth, col : col + LANES]
                spread(wide_ref, j * depth, depth, half, tile, val)
    step = 8

    def body(i, state):
        at = i * step
        one = convolve_short(wide_ref, taps_ref, 1, at, step)
        two = convolve_short(wide_ref, taps_ref, 2, depth + at, step)
        g = (one * two).astype(bf16).astype(f32)
        g_ref[pl.ds(pl.multiple_of(at * 8, 8 * step), 8 * step), :] = g.reshape(step * 8, LANES)
        decay = decay_ref[...]
        for t in range(step):
            state = decay * state + g[t][None]
        return state

    state = lax.fori_loop(0, rows // step, body, jnp.zeros((MODES, 8, LANES), f32))
    e0_ref[...] = state[:, :4]
    e_ref[...] = reach_ref[:, 4:] * state[:, :4] + state[:, 4:]


def gate(rows, *arrays):
    whole = pl.BlockSpec(memory_space=pltpu.VMEM)
    return pl.pallas_call(
        functools.partial(gate_kernel, rows),
        out_shape=[
            jax.ShapeDtypeStruct((rows * 8, LANES), f32),
            jax.ShapeDtypeStruct((MODES, 4, LANES), f32),
            jax.ShapeDtypeStruct((MODES, 4, LANES), f32),
        ],
        in_specs=[whole] * len(arrays),
        out_specs=[whole] * 3,
        scratch_shapes=[pltpu.VMEM((2 * (rows + HALO) * 8, LANES), f32)],
        compiler_params=params(),
        name="gate",
    )(*arrays)


def convolve_kernel(rows, spot_ref, p_ref, g_ref, e0_ref, ends_ref, taps_ref, decay_ref, gain_ref, reach_ref, chip_ref, bypass_ref, mine_ref, theirs_ref, wide_ref, mod_ref):
    step = 8
    depth = rows + HALO
    core, chip = spot_ref[0], spot_ref[1]
    for half in range(2):
        for tile in range(4):
            val = p_ref[half * rows : half * rows + depth, tile * LANES : (tile + 1) * LANES]
            spread(wide_ref, 0, depth, half, tile, val)

    def earlier(i, state):
        return chip_ref[...] * state + ends_ref[i].astype(f32)

    sin = lax.fori_loop(0, chip, earlier, jnp.zeros((MODES, 4, LANES), f32))
    state = reach_ref[...] * jnp.concatenate([sin, sin], axis=1) + jnp.concatenate(
        [jnp.zeros_like(sin), e0_ref[...]], axis=1
    )
    bypass = bypass_ref[...]

    def body(i, state):
        at = i * step
        put = pl.ds(pl.multiple_of(at * 8, 8 * step), 8 * step)
        g = g_ref[put, :].reshape(step, 8, LANES)
        f0 = convolve_short(wide_ref, taps_ref, 0, at, step)
        decay, gain = decay_ref[...], gain_ref[...]
        rows_out = []
        for t in range(step):
            state = decay * state + g[t][None]
            rows_out.append(f0[t] * (jnp.sum(gain * state, axis=0) + bypass * g[t]))
        mod_ref[put, :] = jnp.concatenate(rows_out, axis=0)
        return state

    lax.fori_loop(0, rows // step, body, state)
    for tile in range(4):
        first = mod_ref[pl.ds(tile, rows, stride=8), :].astype(bf16)
        second = mod_ref[pl.ds(4 + tile, rows, stride=8), :].astype(bf16)
        cols = slice(tile * LANES, (tile + 1) * LANES)
        mine_ref[:, cols] = jnp.where(core == 0, first, second)
        theirs_ref[:, cols] = jnp.where(core == 0, second, first)


def convolve(rows, spot, *arrays):
    whole = pl.BlockSpec(memory_space=pltpu.VMEM)
    return pl.pallas_call(
        functools.partial(convolve_kernel, rows),
        out_shape=[jax.ShapeDtypeStruct((rows, 4 * LANES), bf16)] * 2,
        in_specs=[pl.BlockSpec(memory_space=pltpu.SMEM)] + [whole] * len(arrays),
        out_specs=[whole] * 2,
        scratch_shapes=[
            pltpu.VMEM(((rows + HALO) * 8, LANES), f32),
            pltpu.VMEM((rows * 8, LANES), f32),
        ],
        compiler_params=params(),
        name="convolve",
    )(spot, *arrays)


def output_kernel(count, at_ref, mine_ref, theirs_ref, *refs):
    for a, b, out_ref in zip(refs[:count], refs[count : 2 * count], refs[2 * count :]):
        got = jnp.dot(mine_ref[...], a[...], preferred_element_type=f32)
        got = got + jnp.dot(theirs_ref[...], b[...], preferred_element_type=f32)
        out_ref[...] = got.astype(out_ref.dtype)


def output(core, blocks, mine, theirs, weight, dtypes):
    rows, deep = mine.shape
    count = len(blocks)
    wide = 512
    at = jnp.stack([core] + [jnp.asarray(b, jnp.int32) for b in blocks])
    whole = pl.BlockSpec((rows, deep), lambda i, at: (0, 0))
    in_specs = [whole, whole]
    for other in (False, True):
        for b in range(count):
            in_specs.append(
                pl.BlockSpec(
                    (deep, wide),
                    functools.partial(
                        lambda b, other, i, at: (1 - at[0] if other else at[0], at[1 + b]), b, other
                    ),
                )
            )
    return pl.pallas_call(
        functools.partial(output_kernel, count),
        grid_spec=pltpu.PrefetchScalarGridSpec(
            num_scalar_prefetch=1,
            grid=(1,),
            in_specs=in_specs,
            out_specs=[pl.BlockSpec((rows, wide), lambda i, at: (0, 0))] * count,
        ),
        out_shape=[jax.ShapeDtypeStruct((rows, wide), t) for t in dtypes],
        compiler_params=params(),
        cost_estimate=pl.CostEstimate(
            flops=4 * rows * deep * count * wide, bytes_accessed=0, transcendentals=0
        ),
        name="output",
    )(at, mine, theirs, *([weight] * (2 * count)))


def add_kernel(*refs):
    total = refs[0][...].astype(f32)
    for r in refs[1:-1]:
        total = total + r[...].astype(f32)
    refs[-1][...] = total.astype(bf16)


def add(*arrays):
    whole = pl.BlockSpec(memory_space=pltpu.VMEM)
    return pl.pallas_call(
        add_kernel,
        out_shape=jax.ShapeDtypeStruct(arrays[0].shape, bf16),
        in_specs=[whole] * len(arrays),
        out_specs=whole,
        compiler_params=params(),
        name="add",
    )(*arrays)


def finish_kernel(o0, o1, a0, a1, b0, b1, out_ref):
    half = o0.shape[1]
    for cols, parts in ((slice(0, half), (o0, a0, b0)), (slice(half, None), (o1, a1, b1))):
        total = parts[0][...] + parts[1][...].astype(f32) + parts[2][...].astype(f32)
        out_ref[:, cols] = total.astype(bf16)


def finish(*arrays):
    rows, half = arrays[0].shape
    whole = pl.BlockSpec(memory_space=pltpu.VMEM)
    return pl.pallas_call(
        finish_kernel,
        out_shape=jax.ShapeDtypeStruct((rows, 2 * half), bf16),
        in_specs=[whole] * len(arrays),
        out_specs=whole,
        compiler_params=params(),
        name="finish",
    )(*arrays)


def on_device(tokens, norm_gain, in_weight, short_taps, decay_rates, residues, bypass, out_weight):
    rows = tokens.shape[0]
    chans = in_weight.shape[2]
    half = chans // 2
    quarter = half // 2
    core, z, x, chan = (lax.axis_index(a).astype(jnp.int32) for a in ("core", "z", "x", "chan"))
    nz, nx, ny = (lax.axis_size(a) for a in ("z", "x", "chan"))
    core1 = core.reshape(1)

    def of_core(array, axis, which):
        return lax.dynamic_slice_in_dim(array, which * half, half, axis)

    weight = in_weight.transpose(1, 0, 2)
    weight0 = lax.all_gather(weight[:1], ("z", "x", "core"), axis=1, tiled=True)

    pair = weight[1:]
    kept = of_core(pair, 2, core)
    got = shift(of_core(pair, 2, 1 - core), "core", 1)
    first = jnp.where(core == 0, kept, got)
    second = jnp.where(core == 0, got, kept)
    unit = jnp.concatenate([first, second], axis=1)[None]
    unit_a, unit_b = unit[..., :quarter], unit[..., quarter:]

    other = shift(tokens, "core", 1)
    last = jnp.where(core == 1, tokens[rows - HALO :], other[rows - HALO :])
    halo = from_behind(last, ("z", "x"), 1)
    normed = norm(core1, tokens, other, halo, norm_gain)

    def place(dz, dx):
        return ((z + dz) % nz) * nx + (x + dx) % nx

    b = {0: unit_b}
    b[-1], b[1] = shift(b[0], "z", 1), shift(b[0], "z", -1)
    b[-2], b[2] = shift(b[-1], "z", 1), shift(b[1], "z", -1)
    b[-3], b[3] = shift(b[-2], "z", 1), shift(b[2], "z", -1)
    b[4] = shift(b[3], "z", -1)
    a_m1, a_p1, a_p2 = shift(unit_a, "x", 1), shift(unit_a, "x", -1), shift(unit_a, "x", 2)
    a_order = (0, -1, 1, 2)
    a = {0: join([unit_a, a_m1, a_p1, a_p2])}
    a[-1], a[1] = shift(a[0], "z", 1), shift(a[0], "z", -1)
    a[-2], a[2] = shift(a[-1], "z", 1), shift(a[1], "z", -1)
    a[-3], a[3] = shift(a[-2], "z", 1), shift(a[2], "z", -1)
    a4_low = shift(a[-3][:2], "z", 1)
    a4_high = shift(a[3][2:], "z", -1)

    near, far = (0, -1, 1, 2), (-2, -3, 3, 4)
    b_near = join([b[d] for d in near])
    b_far = join([b[d] for d in far], [normed])
    bn_m1, bn_p1 = shift(b_near, "x", 1), shift(b_near, "x", -1)
    bf_m1, bf_p1 = shift(b_far, "x", 1), shift(b_far, "x", -1)
    bn_p2 = shift(bn_m1, "x", 1)
    bf_p2 = shift(bf_p1, "x", -1)

    def a_places(dz):
        return [place(dz, dx) for dx in a_order]

    acc_a = project(normed, None, [a[0]], a_places(0))
    acc_a = project(normed, acc_a, [a[-1], a[1]], a_places(-1) + a_places(1))
    acc_a = project(normed, acc_a, [a[-2], a[2]], a_places(-2) + a_places(2))
    acc_a = project(
        normed, acc_a, [a[-3], a[3], a4_low, a4_high], a_places(-3) + a_places(3) + a_places(4)
    )

    def b_places(zs, dx):
        return [place(dz, dx) for dz in zs]

    acc_b = project(normed, None, [b_near, b_far], b_places(near, 0) + b_places(far, 0))
    acc_b = project(normed, acc_b, [bn_m1, bn_p1], b_places(near, -1) + b_places(near, 1))
    acc_b = project(
        normed,
        acc_b,
        [bf_m1, bf_p1, bn_p2, bf_p2],
        b_places(far, -1) + b_places(far, 1) + b_places(near, 2) + b_places(far, 2),
    )

    def by_tile(array):
        mine = of_core(array, array.ndim - 1, core)
        tiled = mine.reshape(mine.shape[:-1] + (4, LANES))
        return jnp.concatenate([tiled, tiled], axis=-2)

    rates = by_tile(decay_rates)
    gain = by_tile(residues) * jnp.sqrt(-jnp.expm1(-2.0 * rates))
    decay = jnp.exp(-rates)
    halves = (jnp.arange(8) // 4).astype(f32)[None, :, None]
    reach = jnp.exp(-rates * (halves * float(rows)))
    chip_decay = jnp.exp(-rates[:, :4] * float(2 * rows))
    taps = by_tile(short_taps)

    gated, end_first, end = gate(rows, acc_a, acc_b, taps, decay, reach)

    sent = jnp.broadcast_to(end.reshape(1, MODES, half).astype(bf16), (nz * nx, MODES, half))
    ends = lax.all_to_all(sent, ("z", "x"), 0, 0).reshape(nz * nx, MODES, 4, LANES)
    projected0 = project_all(core1, normed, weight0, half)
    spot = jnp.stack([core, z * nx + x])
    mine, to_swap = convolve(
        rows,
        spot,
        projected0,
        gated,
        end_first,
        ends,
        taps,
        decay,
        gain,
        reach,
        chip_decay,
        by_tile(bypass),
    )
    theirs = shift(to_swap, "core", 1)

    def blocks(dy):
        at = ((chan + dy) % ny) * 2
        return [at, at + 1]

    far0, far1 = output(core, blocks(2), mine, theirs, out_weight, [bf16, bf16])
    next0, next1, prev0, prev1 = output(
        core, blocks(1) + blocks(-1), mine, theirs, out_weight, [f32, bf16, bf16, f32]
    )
    own0, own1 = output(core, blocks(0), mine, theirs, out_weight, [f32, f32])
    via0, via1 = shift(far0, "chan", 1), shift(far1, "chan", -1)
    from_prev1, from_next0 = shift(next1, "chan", 1), shift(prev0, "chan", -1)
    from_prev0 = shift(add(next0, via0), "chan", 1)
    from_next1 = shift(add(prev1, via1), "chan", -1)
    return finish(own0, own1, from_prev0, from_prev1, from_next0, from_next1)


def solution(mesh):
    grid = mesh.devices.reshape(8, 4, 2, 4)
    fine = Mesh(grid, ("z", "x", "core", "chan"))
    seq = ("z", "x", "core")
    in_specs = (
        P(seq, None),
        P(),
        P(seq, None, "chan"),
        P(None, None, "chan"),
        P(None, "chan"),
        P(None, "chan"),
        P("chan"),
        P("chan", None),
    )
    return jax.shard_map(
        on_device, mesh=fine, in_specs=in_specs, out_specs=P(seq, "chan"), check_vma=False
    )
```

```python
import functools

import jax
import jax.numpy as jnp
from jax import lax
from jax.experimental import pallas as pl
from jax.experimental.pallas import tpu as pltpu
from jax.sharding import Mesh, PartitionSpec as P

SHORT = 7
MODES = 16
LANES = 128
UNIT = 128
HALO = 16
VMEM = 48 * 1024 * 1024
bf16, f32 = jnp.bfloat16, jnp.float32


def shift(block, axes, distance):
    count = lax.axis_size(axes)
    return lax.ppermute(block, axes, [(i, (i + distance) % count) for i in range(count)])


def from_behind(block, axes, distance):
    count = lax.axis_size(axes)
    return lax.ppermute(block, axes, [(i, i + distance) for i in range(count - distance)])


def params():
    return pltpu.CompilerParams(vmem_limit_bytes=VMEM)


def norm_kernel(core_ref, own_ref, other_ref, halo_ref, gain_ref, out_ref):
    at = pl.program_id(0)
    per_core = (pl.num_programs(0) - 1) // 2

    def put(src, rows):
        wide = src[...].astype(f32)
        mean = jnp.mean(wide * wide, axis=1, keepdims=True)
        out_ref[:rows, :] = (wide * lax.rsqrt(mean + 1e-05) * gain_ref[...]).astype(bf16)

    @pl.when((at < 2 * per_core) & (at // per_core == core_ref[0]))
    def _():
        put(own_ref, own_ref.shape[0])

    @pl.when((at < 2 * per_core) & (at // per_core != core_ref[0]))
    def _():
        put(other_ref, other_ref.shape[0])

    @pl.when(at == 2 * per_core)
    def _():
        put(halo_ref, HALO)


def norm(core, own, other, halo, gain):
    rows, width = own.shape
    block = 128
    per_core = rows // block

    def of_own(i, core):
        return jnp.clip(i - core[0] * per_core, 0, per_core - 1), 0

    def of_other(i, core):
        return jnp.clip(i - (1 - core[0]) * per_core, 0, per_core - 1), 0

    return pl.pallas_call(
        norm_kernel,
        grid_spec=pltpu.PrefetchScalarGridSpec(
            num_scalar_prefetch=1,
            grid=(2 * per_core + 1,),
            in_specs=[
                pl.BlockSpec((block, width), of_own),
                pl.BlockSpec((block, width), of_other),
                pl.BlockSpec((HALO, width), lambda i, core: (0, 0)),
                pl.BlockSpec((1, width), lambda i, core: (0, 0)),
            ],
            out_specs=pl.BlockSpec((block, width), lambda i, core: (i, 0)),
        ),
        out_shape=jax.ShapeDtypeStruct((2 * rows + HALO, width), bf16),
        compiler_params=params(),
        name="norm",
    )(core, own, other, halo, gain.reshape(1, width))


def columns_of(left_ref, places):
    return jnp.concatenate(
        [left_ref[:, pl.ds(pl.multiple_of(p * UNIT, UNIT), UNIT)] for p in places], axis=1
    )


def project_kernel(groups, offs_ref, left_ref, *refs):
    out_ref, refs = refs[-1], refs[:-1]
    at = 0
    total = None
    for count in groups:
        pieces, refs = refs[:count], refs[count:]
        units = sum(p.shape[0] for p in pieces)
        left = columns_of(left_ref, [offs_ref[at + u] for u in range(units)])
        at += units
        right = jnp.concatenate(
            [p[...].reshape(p.shape[0] * UNIT, p.shape[-1]) for p in pieces], axis=0
        )
        got = jnp.dot(left, right, preferred_element_type=f32)
        total = got if total is None else total + got
    out_ref[...] = total


def project(normed, groups, places):
    rows, deep = normed.shape
    pieces = [p for group in groups for p in group]
    width = pieces[0].shape[-1]
    block = 256
    offs = jnp.stack([jnp.asarray(p, jnp.int32) for p in places])
    in_specs = [pl.BlockSpec((rows, deep), lambda j, offs: (0, 0))]
    in_specs += [
        pl.BlockSpec(p.shape[:2] + (block,), lambda j, offs: (0, 0, j)) for p in pieces
    ]
    return pl.pallas_call(
        functools.partial(project_kernel, tuple(len(g) for g in groups)),
        grid_spec=pltpu.PrefetchScalarGridSpec(
            num_scalar_prefetch=1,
            grid=(width // block,),
            in_specs=in_specs,
            out_specs=pl.BlockSpec((rows, block), lambda j, offs: (0, j)),
        ),
        out_shape=jax.ShapeDtypeStruct((rows, width), f32),
        compiler_params=params(),
        cost_estimate=pl.CostEstimate(
            flops=2 * rows * deep * width, bytes_accessed=rows * deep * 2, transcendentals=0
        ),
        name="project",
    )(offs, normed, *pieces)


def join_kernel(count, *refs):
    at = 0
    for src in refs[:count]:
        units = src.shape[0] if len(src.shape) == 3 else 1
        refs[-1][at : at + units] = src[...].reshape((units,) + src.shape[-2:])
        at += units


def join(pieces, after=()):
    whole = pl.BlockSpec(memory_space=pltpu.VMEM)
    units = sum(p.shape[0] if p.ndim == 3 else 1 for p in pieces)
    return pl.pallas_call(
        functools.partial(join_kernel, len(pieces)),
        out_shape=jax.ShapeDtypeStruct((units,) + pieces[0].shape[-2:], bf16),
        in_specs=[whole] * len(pieces) + [pl.BlockSpec(memory_space=pl.ANY)] * len(after),
        out_specs=whole,
        compiler_params=params(),
        name="join",
    )(*pieces, *after)


def project_all_kernel(core_ref, left_ref, right_ref, out_ref):
    out_ref[...] = jnp.dot(left_ref[...], right_ref[...], preferred_element_type=f32)


def project_all(core, normed, weight, width):
    rows, deep = normed.shape
    block = 256
    per_core = width // block
    return pl.pallas_call(
        project_all_kernel,
        grid_spec=pltpu.PrefetchScalarGridSpec(
            num_scalar_prefetch=1,
            grid=(per_core,),
            in_specs=[
                pl.BlockSpec((rows, deep), lambda j, core: (0, 0)),
                pl.BlockSpec((deep, block), lambda j, core: (0, core[0] * per_core + j)),
            ],
            out_specs=pl.BlockSpec((rows, block), lambda j, core: (0, j)),
        ),
        out_shape=jax.ShapeDtypeStruct((rows, width), f32),
        compiler_params=params(),
        cost_estimate=pl.CostEstimate(
            flops=2 * rows * deep * width, bytes_accessed=rows * deep * 2, transcendentals=0
        ),
        name="project_all",
    )(core, normed, weight)


def spread(wide_ref, at, rows, srcs):
    def put(first, half, tile, count, val):
        to = pl.ds((at + first) * 8 + half * 4 + tile, count, stride=8)
        wide_ref[to, :] = val.astype(bf16).astype(f32)

    for tile, (src_ref, col) in enumerate(srcs):
        cols = slice(col, col + LANES)
        put(0, 0, tile, HALO, src_ref[2 * rows : 2 * rows + HALO, cols])
        put(HALO, 0, tile, rows, src_ref[:rows, cols])
        put(0, 1, tile, rows + HALO, src_ref[rows - HALO : 2 * rows, cols])


def convolve_short(wide_ref, taps_ref, j, base, step):
    reach = step + SHORT - 1
    rows = pl.ds(pl.multiple_of((base + HALO - (SHORT - 1)) * 8, 8), reach * 8)
    x = wide_ref[rows, :].reshape(reach, 8, LANES)
    total = taps_ref[j, 0][None] * x[SHORT - 1 : SHORT - 1 + step]
    for i in range(1, SHORT):
        total = total + taps_ref[j, i][None] * x[SHORT - 1 - i : SHORT - 1 - i + step]
    return total


def gate_kernel(rows, _, a_ref, b_ref, taps_ref, decay_ref, reach_ref, g_ref, e0_ref, e_ref, wide_ref):
    depth = rows + HALO
    for j in range(2):
        cols = 2 * j * LANES, (2 * j + 1) * LANES
        srcs = [(a_ref, c) for c in cols] + [(b_ref, c) for c in cols]
        spread(wide_ref, j * depth, rows, srcs)
    step = 8

    def body(i, state):
        at = i * step
        one = convolve_short(wide_ref, taps_ref, 1, at, step)
        two = convolve_short(wide_ref, taps_ref, 2, depth + at, step)
        g = (one * two).astype(bf16).astype(f32)
        g_ref[pl.ds(pl.multiple_of(at * 8, 8 * step), 8 * step), :] = g.reshape(step * 8, LANES)
        decay = decay_ref[...]
        for t in range(step):
            state = decay * state + g[t][None]
        return state

    state = lax.fori_loop(0, rows // step, body, jnp.zeros((MODES, 8, LANES), f32))
    e0_ref[...] = state[:, :4]
    e_ref[...] = reach_ref[:, 4:] * state[:, :4] + state[:, 4:]


def gate(rows, after, *arrays):
    whole = pl.BlockSpec(memory_space=pltpu.VMEM)
    return pl.pallas_call(
        functools.partial(gate_kernel, rows),
        out_shape=[
            jax.ShapeDtypeStruct((rows * 8, LANES), f32),
            jax.ShapeDtypeStruct((MODES, 4, LANES), f32),
            jax.ShapeDtypeStruct((MODES, 4, LANES), f32),
        ],
        in_specs=[pl.BlockSpec(memory_space=pl.ANY)] + [whole] * len(arrays),
        out_specs=[whole] * 3,
        scratch_shapes=[pltpu.VMEM((2 * (rows + HALO) * 8, LANES), f32)],
        compiler_params=params(),
        name="gate",
    )(after, *arrays)


def convolve_kernel(rows, spot_ref, p_ref, g_ref, e0_ref, ends_ref, taps_ref, decay_ref, gain_ref, reach_ref, chip_ref, bypass_ref, mine_ref, theirs_ref, wide_ref, mod_ref):
    step = 8
    core, chip = spot_ref[0], spot_ref[1]
    spread(wide_ref, 0, rows, [(p_ref, tile * LANES) for tile in range(4)])

    def earlier(i, state):
        return chip_ref[...] * state + ends_ref[i].astype(f32)

    sin = lax.fori_loop(0, chip, earlier, jnp.zeros((MODES, 4, LANES), f32))
    state = reach_ref[...] * jnp.concatenate([sin, sin], axis=1) + jnp.concatenate(
        [jnp.zeros_like(sin), e0_ref[...]], axis=1
    )
    bypass = bypass_ref[...]

    def body(i, state):
        at = i * step
        put = pl.ds(pl.multiple_of(at * 8, 8 * step), 8 * step)
        g = g_ref[put, :].reshape(step, 8, LANES)
        f0 = convolve_short(wide_ref, taps_ref, 0, at, step)
        decay, gain = decay_ref[...], gain_ref[...]
        rows_out = []
        for t in range(step):
            state = decay * state + g[t][None]
            rows_out.append(f0[t] * (jnp.sum(gain * state, axis=0) + bypass * g[t]))
        mod_ref[put, :] = jnp.concatenate(rows_out, axis=0)
        return state

    lax.fori_loop(0, rows // step, body, state)
    for tile in range(4):
        first = mod_ref[pl.ds(tile, rows, stride=8), :].astype(bf16)
        second = mod_ref[pl.ds(4 + tile, rows, stride=8), :].astype(bf16)
        cols = slice(tile * LANES, (tile + 1) * LANES)
        mine_ref[:, cols] = jnp.where(core == 0, first, second)
        theirs_ref[:, cols] = jnp.where(core == 0, second, first)


def convolve(rows, spot, *arrays):
    whole = pl.BlockSpec(memory_space=pltpu.VMEM)
    return pl.pallas_call(
        functools.partial(convolve_kernel, rows),
        out_shape=[jax.ShapeDtypeStruct((rows, 4 * LANES), bf16)] * 2,
        in_specs=[pl.BlockSpec(memory_space=pltpu.SMEM)] + [whole] * len(arrays),
        out_specs=[whole] * 2,
        scratch_shapes=[
            pltpu.VMEM(((rows + HALO) * 8, LANES), f32),
            pltpu.VMEM((rows * 8, LANES), f32),
        ],
        compiler_params=params(),
        name="convolve",
    )(spot, *arrays)


def output_kernel(count, at_ref, mine_ref, theirs_ref, *refs):
    for a, b, out_ref in zip(refs[:count], refs[count : 2 * count], refs[2 * count :]):
        got = jnp.dot(mine_ref[...], a[...], preferred_element_type=f32)
        got = got + jnp.dot(theirs_ref[...], b[...], preferred_element_type=f32)
        out_ref[...] = got.astype(out_ref.dtype)


def output(core, blocks, mine, theirs, weight, dtypes):
    rows, deep = mine.shape
    count = len(blocks)
    wide = 512
    at = jnp.stack([core] + [jnp.asarray(b, jnp.int32) for b in blocks])
    whole = pl.BlockSpec((rows, deep), lambda i, at: (0, 0))
    in_specs = [whole, whole]
    for other in (False, True):
        for b in range(count):
            in_specs.append(
                pl.BlockSpec(
                    (deep, wide),
                    functools.partial(
                        lambda b, other, i, at: (1 - at[0] if other else at[0], at[1 + b]), b, other
                    ),
                )
            )
    return pl.pallas_call(
        functools.partial(output_kernel, count),
        grid_spec=pltpu.PrefetchScalarGridSpec(
            num_scalar_prefetch=1,
            grid=(1,),
            in_specs=in_specs,
            out_specs=[pl.BlockSpec((rows, wide), lambda i, at: (0, 0))] * count,
        ),
        out_shape=[jax.ShapeDtypeStruct((rows, wide), t) for t in dtypes],
        compiler_params=params(),
        cost_estimate=pl.CostEstimate(
            flops=4 * rows * deep * count * wide, bytes_accessed=0, transcendentals=0
        ),
        name="output",
    )(at, mine, theirs, *([weight] * (2 * count)))


def add_kernel(*refs):
    total = refs[0][...].astype(f32)
    for r in refs[1:-1]:
        total = total + r[...].astype(f32)
    refs[-1][...] = total.astype(bf16)


def add(*arrays):
    whole = pl.BlockSpec(memory_space=pltpu.VMEM)
    return pl.pallas_call(
        add_kernel,
        out_shape=jax.ShapeDtypeStruct(arrays[0].shape, bf16),
        in_specs=[whole] * len(arrays),
        out_specs=whole,
        compiler_params=params(),
        name="add",
    )(*arrays)


def finish_kernel(o0, o1, a0, a1, b0, b1, out_ref):
    half = o0.shape[1]
    for cols, parts in ((slice(0, half), (o0, a0, b0)), (slice(half, None), (o1, a1, b1))):
        total = parts[0][...] + parts[1][...].astype(f32) + parts[2][...].astype(f32)
        out_ref[:, cols] = total.astype(bf16)


def finish(*arrays):
    rows, half = arrays[0].shape
    whole = pl.BlockSpec(memory_space=pltpu.VMEM)
    return pl.pallas_call(
        finish_kernel,
        out_shape=jax.ShapeDtypeStruct((rows, 2 * half), bf16),
        in_specs=[whole] * len(arrays),
        out_specs=whole,
        compiler_params=params(),
        name="finish",
    )(*arrays)


def on_device(tokens, norm_gain, in_weight, short_taps, decay_rates, residues, bypass, out_weight):
    rows = tokens.shape[0]
    chans = in_weight.shape[2]
    half = chans // 2
    quarter = half // 2
    core, z, x, chan = (lax.axis_index(a).astype(jnp.int32) for a in ("core", "z", "x", "chan"))
    nz, nx, ny = (lax.axis_size(a) for a in ("z", "x", "chan"))
    core1 = core.reshape(1)

    def of_core(array, axis, which):
        return lax.dynamic_slice_in_dim(array, which * half, half, axis)

    weight = in_weight.transpose(1, 0, 2)
    weight0 = lax.all_gather(weight[0], ("z", "x", "core"), axis=0, tiled=True)

    def streams(which):
        return lax.dynamic_slice(weight, (1, 0, which * half), (2, weight.shape[1], half))

    kept = streams(core)
    got = shift(streams(1 - core), "core", 1)
    first = jnp.where(core == 0, kept, got)
    second = jnp.where(core == 0, got, kept)
    unit = jnp.concatenate([first, second], axis=1)
    unit_a = jnp.concatenate([unit[0][:, :quarter], unit[1][:, :quarter]], axis=1)
    unit_b = jnp.concatenate([unit[0][:, quarter:], unit[1][:, quarter:]], axis=1)

    other = shift(tokens, "core", 1)
    last = jnp.where(core == 1, tokens[rows - HALO :], other[rows - HALO :])
    halo = from_behind(last, ("z", "x"), 1)
    normed = norm(core1, tokens, other, halo, norm_gain)

    def place(dz, dx):
        return ((z + dz) % nz) * nx + (x + dx) % nx

    b = {0: unit_b}
    b[-1], b[1] = shift(b[0], "z", 1), shift(b[0], "z", -1)
    b[-2], b[2] = shift(b[-1], "z", 1), shift(b[1], "z", -1)
    b[-3], b[3] = shift(b[-2], "z", 1), shift(b[2], "z", -1)
    b[4] = shift(b[3], "z", -1)
    a_m1, a_p1, a_p2 = shift(unit_a, "x", 1), shift(unit_a, "x", -1), shift(unit_a, "x", 2)
    a = {0: join([unit_a, a_m1, a_p1, a_p2])}
    a[-1], a[1] = shift(a[0], "z", 1), shift(a[0], "z", -1)
    a[-2], a[2] = shift(a[-1], "z", 1), shift(a[1], "z", -1)
    a[-3], a[3] = shift(a[-2], "z", 1), shift(a[2], "z", -1)
    a4_low = shift(a[-3][:2], "z", 1)
    a4_high = shift(a[3][2:], "z", -1)

    near, far = (0, -1, 1, 2), (-2, -3, 3, 4)
    b_near = join([b[d] for d in near], [normed])
    bn_m1, bn_p1 = shift(b_near, "x", 1), shift(b_near, "x", -1)
    b_far = join([b[d] for d in far], [bn_m1, bn_p1])
    bf_m1, bf_p1 = shift(b_far, "x", 1), shift(b_far, "x", -1)
    bn_p2 = shift(bn_m1, "x", 1)
    bf_p2 = shift(join([bf_p1], [bf_m1]), "x", -1)

    projected_a = project(
        normed,
        [(a[0], a[-1]), (a[1], a[-2]), (a[2], a[-3]), (a[3], a4_low, a4_high)],
        [place(dz, dx) for dz in (0, -1, 1, -2, 2, -3, 3, 4) for dx in (0, -1, 1, 2)],
    )
    projected_b = project(
        normed,
        [(b_near, b_far), (bn_m1, bf_m1), (bn_p1, bf_p1), (bn_p2, bf_p2)],
        [place(dz, dx) for dx in (0, -1, 1, 2) for dz in near + far],
    )

    def by_tile(array):
        mine = of_core(array, array.ndim - 1, core)
        tiled = mine.reshape(mine.shape[:-1] + (4, LANES))
        return jnp.concatenate([tiled, tiled], axis=-2)

    rates = by_tile(decay_rates)
    gain = by_tile(residues) * jnp.sqrt(-jnp.expm1(-2.0 * rates))
    decay = jnp.exp(-rates)
    halves = (jnp.arange(8) // 4).astype(f32)[None, :, None]
    reach = jnp.exp(-rates * (halves * float(rows)))
    chip_decay = jnp.exp(-rates[:, :4] * float(2 * rows))
    taps = by_tile(short_taps)

    gated, end_first, end = gate(rows, weight0, projected_a, projected_b, taps, decay, reach)

    sent = jnp.broadcast_to(end.reshape(1, MODES, half).astype(bf16), (nz * nx, MODES, half))
    ends = lax.all_to_all(sent, ("z", "x"), 0, 0).reshape(nz * nx, MODES, 4, LANES)
    projected0 = project_all(core1, normed, weight0, half)
    spot = jnp.stack([core, z * nx + x])
    mine, to_swap = convolve(
        rows,
        spot,
        projected0,
        gated,
        end_first,
        ends,
        taps,
        decay,
        gain,
        reach,
        chip_decay,
        by_tile(bypass),
    )
    theirs = shift(to_swap, "core", 1)

    def blocks(dy):
        at = ((chan + dy) % ny) * 2
        return [at, at + 1]

    far0, far1 = output(core, blocks(2), mine, theirs, out_weight, [bf16, bf16])
    next0, next1, prev0, prev1 = output(
        core, blocks(1) + blocks(-1), mine, theirs, out_weight, [f32, bf16, bf16, f32]
    )
    own0, own1 = output(core, blocks(0), mine, theirs, out_weight, [f32, f32])
    via0, via1 = shift(far0, "chan", 1), shift(far1, "chan", -1)
    from_prev1, from_next0 = shift(next1, "chan", 1), shift(prev0, "chan", -1)
    from_prev0 = shift(add(next0, via0), "chan", 1)
    from_next1 = shift(add(prev1, via1), "chan", -1)
    return finish(own0, own1, from_prev0, from_prev1, from_next0, from_next1)


def solution(mesh):
    grid = mesh.devices.reshape(8, 4, 2, 4)
    fine = Mesh(grid, ("z", "x", "core", "chan"))
    seq = ("z", "x", "core")
    in_specs = (
        P(seq, None),
        P(),
        P(seq, None, "chan"),
        P(None, None, "chan"),
        P(None, "chan"),
        P(None, "chan"),
        P("chan"),
        P("chan", None),
    )
    return jax.shard_map(
        on_device, mesh=fine, in_specs=in_specs, out_specs=P(seq, "chan"), check_vma=False
    )
```

```python
import functools

import jax
import jax.numpy as jnp
from jax import lax
from jax.experimental import pallas as pl
from jax.experimental.pallas import tpu as pltpu
from jax.sharding import Mesh, PartitionSpec as P

SHORT = 7
MODES = 16
LANES = 128
UNIT = 128
HALO = 16
VMEM = 48 * 1024 * 1024
bf16, f32 = jnp.bfloat16, jnp.float32


def shift(block, axes, distance):
    count = lax.axis_size(axes)
    return lax.ppermute(block, axes, [(i, (i + distance) % count) for i in range(count)])


def from_behind(block, axes, distance):
    count = lax.axis_size(axes)
    return lax.ppermute(block, axes, [(i, i + distance) for i in range(count - distance)])


def params():
    return pltpu.CompilerParams(vmem_limit_bytes=VMEM)


def norm_kernel(core_ref, own_ref, other_ref, halo_ref, gain_ref, out_ref):
    at = pl.program_id(0)
    per_core = (pl.num_programs(0) - 1) // 2

    def put(src, rows):
        wide = src[...].astype(f32)
        mean = jnp.mean(wide * wide, axis=1, keepdims=True)
        out_ref[:rows, :] = (wide * lax.rsqrt(mean + 1e-05) * gain_ref[...]).astype(bf16)

    @pl.when((at < 2 * per_core) & (at // per_core == core_ref[0]))
    def _():
        put(own_ref, own_ref.shape[0])

    @pl.when((at < 2 * per_core) & (at // per_core != core_ref[0]))
    def _():
        put(other_ref, other_ref.shape[0])

    @pl.when(at == 2 * per_core)
    def _():
        put(halo_ref, HALO)


def norm(core, own, other, halo, gain):
    rows, width = own.shape
    block = 128
    per_core = rows // block

    def of_own(i, core):
        return jnp.clip(i - core[0] * per_core, 0, per_core - 1), 0

    def of_other(i, core):
        return jnp.clip(i - (1 - core[0]) * per_core, 0, per_core - 1), 0

    return pl.pallas_call(
        norm_kernel,
        grid_spec=pltpu.PrefetchScalarGridSpec(
            num_scalar_prefetch=1,
            grid=(2 * per_core + 1,),
            in_specs=[
                pl.BlockSpec((block, width), of_own),
                pl.BlockSpec((block, width), of_other),
                pl.BlockSpec((HALO, width), lambda i, core: (0, 0)),
                pl.BlockSpec((1, width), lambda i, core: (0, 0)),
            ],
            out_specs=pl.BlockSpec((block, width), lambda i, core: (i, 0)),
        ),
        out_shape=jax.ShapeDtypeStruct((2 * rows + HALO, width), bf16),
        compiler_params=params(),
        name="norm",
    )(core, own, other, halo, gain.reshape(1, width))


def columns_of(left_ref, places):
    return jnp.concatenate(
        [left_ref[:, pl.ds(pl.multiple_of(p * UNIT, UNIT), UNIT)] for p in places], axis=1
    )


def project_kernel(groups, offs_ref, left_ref, *refs):
    out_ref, refs = refs[-1], refs[:-1]
    at = 0
    total = None
    for count in groups:
        pieces, refs = refs[:count], refs[count:]
        units = sum(p.shape[0] for p in pieces)
        left = columns_of(left_ref, [offs_ref[at + u] for u in range(units)])
        at += units
        right = jnp.concatenate(
            [p[...].reshape(p.shape[0] * UNIT, p.shape[-1]) for p in pieces], axis=0
        )
        got = jnp.dot(left, right, preferred_element_type=f32)
        total = got if total is None else total + got
    out_ref[...] = total


def project(normed, groups, places):
    rows, deep = normed.shape
    pieces = [p for group in groups for p in group]
    width = pieces[0].shape[-1]
    block = 256
    offs = jnp.stack([jnp.asarray(p, jnp.int32) for p in places])
    in_specs = [pl.BlockSpec((rows, deep), lambda j, offs: (0, 0))]
    in_specs += [
        pl.BlockSpec(p.shape[:2] + (block,), lambda j, offs: (0, 0, j)) for p in pieces
    ]
    return pl.pallas_call(
        functools.partial(project_kernel, tuple(len(g) for g in groups)),
        grid_spec=pltpu.PrefetchScalarGridSpec(
            num_scalar_prefetch=1,
            grid=(width // block,),
            in_specs=in_specs,
            out_specs=pl.BlockSpec((rows, block), lambda j, offs: (0, j)),
        ),
        out_shape=jax.ShapeDtypeStruct((rows, width), f32),
        compiler_params=params(),
        cost_estimate=pl.CostEstimate(
            flops=2 * rows * deep * width, bytes_accessed=rows * deep * 2, transcendentals=0
        ),
        name="project",
    )(offs, normed, *pieces)


def join_kernel(count, *refs):
    at = 0
    for src in refs[:count]:
        units = src.shape[0] if len(src.shape) == 3 else 1
        refs[-1][at : at + units] = src[...].reshape((units,) + src.shape[-2:])
        at += units


def join(pieces, after=()):
    whole = pl.BlockSpec(memory_space=pltpu.VMEM)
    units = sum(p.shape[0] if p.ndim == 3 else 1 for p in pieces)
    return pl.pallas_call(
        functools.partial(join_kernel, len(pieces)),
        out_shape=jax.ShapeDtypeStruct((units,) + pieces[0].shape[-2:], bf16),
        in_specs=[whole] * len(pieces) + [pl.BlockSpec(memory_space=pl.ANY)] * len(after),
        out_specs=whole,
        compiler_params=params(),
        name="join",
    )(*pieces, *after)


def project_all_kernel(core_ref, left_ref, right_ref, out_ref):
    out_ref[...] = jnp.dot(left_ref[...], right_ref[...], preferred_element_type=f32)


def project_all(core, normed, weight, width):
    rows, deep = normed.shape
    block = 256
    per_core = width // block
    return pl.pallas_call(
        project_all_kernel,
        grid_spec=pltpu.PrefetchScalarGridSpec(
            num_scalar_prefetch=1,
            grid=(per_core,),
            in_specs=[
                pl.BlockSpec((rows, deep), lambda j, core: (0, 0)),
                pl.BlockSpec((deep, block), lambda j, core: (0, core[0] * per_core + j)),
            ],
            out_specs=pl.BlockSpec((rows, block), lambda j, core: (0, j)),
        ),
        out_shape=jax.ShapeDtypeStruct((rows, width), f32),
        compiler_params=params(),
        cost_estimate=pl.CostEstimate(
            flops=2 * rows * deep * width, bytes_accessed=rows * deep * 2, transcendentals=0
        ),
        name="project_all",
    )(core, normed, weight)


def spread(wide_ref, at, rows, srcs):
    def put(first, half, tile, count, val):
        to = pl.ds((at + first) * 8 + half * 4 + tile, count, stride=8)
        wide_ref[to, :] = val.astype(bf16).astype(f32)

    for tile, (src_ref, col) in enumerate(srcs):
        cols = slice(col, col + LANES)
        put(0, 0, tile, HALO, src_ref[2 * rows : 2 * rows + HALO, cols])
        put(HALO, 0, tile, rows, src_ref[:rows, cols])
        put(0, 1, tile, rows + HALO, src_ref[rows - HALO : 2 * rows, cols])


def convolve_short(wide_ref, taps_ref, j, base, step):
    reach = step + SHORT - 1
    rows = pl.ds(pl.multiple_of((base + HALO - (SHORT - 1)) * 8, 8), reach * 8)
    x = wide_ref[rows, :].reshape(reach, 8, LANES)
    total = taps_ref[j, 0][None] * x[SHORT - 1 : SHORT - 1 + step]
    for i in range(1, SHORT):
        total = total + taps_ref[j, i][None] * x[SHORT - 1 - i : SHORT - 1 - i + step]
    return total


def gate_kernel(rows, _, a_ref, b_ref, taps_ref, decay_ref, reach_ref, g_ref, e0_ref, e_ref, wide_ref):
    depth = rows + HALO
    for j in range(2):
        cols = 2 * j * LANES, (2 * j + 1) * LANES
        srcs = [(a_ref, c) for c in cols] + [(b_ref, c) for c in cols]
        spread(wide_ref, j * depth, rows, srcs)
    step = 8

    def body(i, state):
        at = i * step
        one = convolve_short(wide_ref, taps_ref, 1, at, step)
        two = convolve_short(wide_ref, taps_ref, 2, depth + at, step)
        g = (one * two).astype(bf16).astype(f32)
        g_ref[pl.ds(pl.multiple_of(at * 8, 8 * step), 8 * step), :] = g.reshape(step * 8, LANES)
        decay = decay_ref[...]
        for t in range(step):
            state = decay * state + g[t][None]
        return state

    state = lax.fori_loop(0, rows // step, body, jnp.zeros((MODES, 8, LANES), f32))
    e0_ref[...] = state[:, :4]
    e_ref[...] = reach_ref[:, 4:] * state[:, :4] + state[:, 4:]


def gate(rows, after, *arrays):
    whole = pl.BlockSpec(memory_space=pltpu.VMEM)
    return pl.pallas_call(
        functools.partial(gate_kernel, rows),
        out_shape=[
            jax.ShapeDtypeStruct((rows * 8, LANES), f32),
            jax.ShapeDtypeStruct((MODES, 4, LANES), f32),
            jax.ShapeDtypeStruct((MODES, 4, LANES), f32),
        ],
        in_specs=[pl.BlockSpec(memory_space=pl.ANY)] + [whole] * len(arrays),
        out_specs=[whole] * 3,
        scratch_shapes=[pltpu.VMEM((2 * (rows + HALO) * 8, LANES), f32)],
        compiler_params=params(),
        name="gate",
    )(after, *arrays)


def feature_kernel(rows, p_ref, taps_ref, f0_ref, wide_ref):
    spread(wide_ref, 0, rows, [(p_ref, tile * LANES) for tile in range(4)])
    step = 8

    def body(i, _):
        at = i * step
        f0 = convolve_short(wide_ref, taps_ref, 0, at, step)
        f0_ref[pl.ds(pl.multiple_of(at * 8, 8 * step), 8 * step), :] = f0.reshape(step * 8, LANES)
        return 0

    lax.fori_loop(0, rows // step, body, 0)


def feature(rows, projected, taps):
    whole = pl.BlockSpec(memory_space=pltpu.VMEM)
    return pl.pallas_call(
        functools.partial(feature_kernel, rows),
        out_shape=jax.ShapeDtypeStruct((rows * 8, LANES), f32),
        in_specs=[whole] * 2,
        out_specs=whole,
        scratch_shapes=[pltpu.VMEM(((rows + HALO) * 8, LANES), f32)],
        compiler_params=params(),
        name="feature",
    )(projected, taps)


def convolve_kernel(rows, spot_ref, f0_ref, g_ref, e0_ref, ends_ref, decay_ref, gain_ref, reach_ref, chip_ref, bypass_ref, mine_ref, theirs_ref, mod_ref):
    step = 8
    core, chip = spot_ref[0], spot_ref[1]

    def earlier(i, state):
        return chip_ref[...] * state + ends_ref[i].astype(f32)

    sin = lax.fori_loop(0, chip, earlier, jnp.zeros((MODES, 4, LANES), f32))
    state = reach_ref[...] * jnp.concatenate([sin, sin], axis=1) + jnp.concatenate(
        [jnp.zeros_like(sin), e0_ref[...]], axis=1
    )
    bypass = bypass_ref[...]

    def body(i, state):
        at = i * step
        put = pl.ds(pl.multiple_of(at * 8, 8 * step), 8 * step)
        g = g_ref[put, :].reshape(step, 8, LANES)
        f0 = f0_ref[put, :].reshape(step, 8, LANES)
        decay, gain = decay_ref[...], gain_ref[...]
        rows_out = []
        for t in range(step):
            state = decay * state + g[t][None]
            rows_out.append(f0[t] * (jnp.sum(gain * state, axis=0) + bypass * g[t]))
        mod_ref[put, :] = jnp.concatenate(rows_out, axis=0)
        return state

    lax.fori_loop(0, rows // step, body, state)
    for tile in range(4):
        first = mod_ref[pl.ds(tile, rows, stride=8), :].astype(bf16)
        second = mod_ref[pl.ds(4 + tile, rows, stride=8), :].astype(bf16)
        cols = slice(tile * LANES, (tile + 1) * LANES)
        mine_ref[:, cols] = jnp.where(core == 0, first, second)
        theirs_ref[:, cols] = jnp.where(core == 0, second, first)


def convolve(rows, spot, *arrays):
    whole = pl.BlockSpec(memory_space=pltpu.VMEM)
    return pl.pallas_call(
        functools.partial(convolve_kernel, rows),
        out_shape=[jax.ShapeDtypeStruct((rows, 4 * LANES), bf16)] * 2,
        in_specs=[pl.BlockSpec(memory_space=pltpu.SMEM)] + [whole] * len(arrays),
        out_specs=[whole] * 2,
        scratch_shapes=[pltpu.VMEM((rows * 8, LANES), f32)],
        compiler_params=params(),
        name="convolve",
    )(spot, *arrays)


def output_kernel(count, at_ref, mine_ref, theirs_ref, *refs):
    for a, b, out_ref in zip(refs[:count], refs[count : 2 * count], refs[2 * count :]):
        got = jnp.dot(mine_ref[...], a[...], preferred_element_type=f32)
        got = got + jnp.dot(theirs_ref[...], b[...], preferred_element_type=f32)
        out_ref[...] = got.astype(out_ref.dtype)


def output(core, blocks, mine, theirs, weight, dtypes):
    rows, deep = mine.shape
    count = len(blocks)
    wide = 512
    at = jnp.stack([core] + [jnp.asarray(b, jnp.int32) for b in blocks])
    whole = pl.BlockSpec((rows, deep), lambda i, at: (0, 0))
    in_specs = [whole, whole]
    for other in (False, True):
        for b in range(count):
            in_specs.append(
                pl.BlockSpec(
                    (deep, wide),
                    functools.partial(
                        lambda b, other, i, at: (1 - at[0] if other else at[0], at[1 + b]), b, other
                    ),
                )
            )
    return pl.pallas_call(
        functools.partial(output_kernel, count),
        grid_spec=pltpu.PrefetchScalarGridSpec(
            num_scalar_prefetch=1,
            grid=(1,),
            in_specs=in_specs,
            out_specs=[pl.BlockSpec((rows, wide), lambda i, at: (0, 0))] * count,
        ),
        out_shape=[jax.ShapeDtypeStruct((rows, wide), t) for t in dtypes],
        compiler_params=params(),
        cost_estimate=pl.CostEstimate(
            flops=4 * rows * deep * count * wide, bytes_accessed=0, transcendentals=0
        ),
        name="output",
    )(at, mine, theirs, *([weight] * (2 * count)))


def add_kernel(*refs):
    total = refs[0][...].astype(f32)
    for r in refs[1:-1]:
        total = total + r[...].astype(f32)
    refs[-1][...] = total.astype(bf16)


def add(*arrays):
    whole = pl.BlockSpec(memory_space=pltpu.VMEM)
    return pl.pallas_call(
        add_kernel,
        out_shape=jax.ShapeDtypeStruct(arrays[0].shape, bf16),
        in_specs=[whole] * len(arrays),
        out_specs=whole,
        compiler_params=params(),
        name="add",
    )(*arrays)


def finish_kernel(o0, o1, a0, a1, b0, b1, out_ref):
    half = o0.shape[1]
    for cols, parts in ((slice(0, half), (o0, a0, b0)), (slice(half, None), (o1, a1, b1))):
        total = parts[0][...] + parts[1][...].astype(f32) + parts[2][...].astype(f32)
        out_ref[:, cols] = total.astype(bf16)


def finish(*arrays):
    rows, half = arrays[0].shape
    whole = pl.BlockSpec(memory_space=pltpu.VMEM)
    return pl.pallas_call(
        finish_kernel,
        out_shape=jax.ShapeDtypeStruct((rows, 2 * half), bf16),
        in_specs=[whole] * len(arrays),
        out_specs=whole,
        compiler_params=params(),
        name="finish",
    )(*arrays)


def on_device(tokens, norm_gain, in_weight, short_taps, decay_rates, residues, bypass, out_weight):
    rows = tokens.shape[0]
    chans = in_weight.shape[2]
    half = chans // 2
    quarter = half // 2
    core, z, x, chan = (lax.axis_index(a).astype(jnp.int32) for a in ("core", "z", "x", "chan"))
    nz, nx, ny = (lax.axis_size(a) for a in ("z", "x", "chan"))
    core1 = core.reshape(1)

    def of_core(array, axis, which):
        return lax.dynamic_slice_in_dim(array, which * half, half, axis)

    weight = in_weight.transpose(1, 0, 2)
    weight0 = lax.all_gather(weight[0], ("z", "x", "core"), axis=0, tiled=True)

    def streams(which):
        return lax.dynamic_slice(weight, (1, 0, which * half), (2, weight.shape[1], half))

    kept = streams(core)
    got = shift(streams(1 - core), "core", 1)
    first = jnp.where(core == 0, kept, got)
    second = jnp.where(core == 0, got, kept)
    unit = jnp.concatenate([first, second], axis=1)
    unit_a = jnp.concatenate([unit[0][:, :quarter], unit[1][:, :quarter]], axis=1)
    unit_b = jnp.concatenate([unit[0][:, quarter:], unit[1][:, quarter:]], axis=1)

    other = shift(tokens, "core", 1)
    last = jnp.where(core == 1, tokens[rows - HALO :], other[rows - HALO :])
    halo = from_behind(last, ("z", "x"), 1)
    normed = norm(core1, tokens, other, halo, norm_gain)

    def place(dz, dx):
        return ((z + dz) % nz) * nx + (x + dx) % nx

    b = {0: unit_b}
    b[-1], b[1] = shift(b[0], "z", 1), shift(b[0], "z", -1)
    b[-2], b[2] = shift(b[-1], "z", 1), shift(b[1], "z", -1)
    b[-3], b[3] = shift(b[-2], "z", 1), shift(b[2], "z", -1)
    b[4] = shift(b[3], "z", -1)
    a_m1, a_p1, a_p2 = shift(unit_a, "x", 1), shift(unit_a, "x", -1), shift(unit_a, "x", 2)
    a = {0: join([unit_a, a_m1, a_p1, a_p2])}
    a[-1], a[1] = shift(a[0], "z", 1), shift(a[0], "z", -1)
    a[-2], a[2] = shift(a[-1], "z", 1), shift(a[1], "z", -1)
    a[-3], a[3] = shift(a[-2], "z", 1), shift(a[2], "z", -1)
    a4_low = shift(a[-3][:2], "z", 1)
    a4_high = shift(a[3][2:], "z", -1)

    near, far = (0, -1, 1, 2), (-2, -3, 3, 4)
    b_near = join([b[d] for d in near], [normed])
    bn_m1, bn_p1 = shift(b_near, "x", 1), shift(b_near, "x", -1)
    b_far = join([b[d] for d in far], [bn_m1, bn_p1])
    bf_m1, bf_p1 = shift(b_far, "x", 1), shift(b_far, "x", -1)
    bn_p2 = shift(bn_m1, "x", 1)
    bf_p2 = shift(join([bf_p1], [bf_m1]), "x", -1)

    projected_a = project(
        normed,
        [(a[0], a[-1]), (a[1], a[-2]), (a[2], a[-3]), (a[3], a4_low, a4_high)],
        [place(dz, dx) for dz in (0, -1, 1, -2, 2, -3, 3, 4) for dx in (0, -1, 1, 2)],
    )
    projected_b = project(
        normed,
        [(b_near, b_far), (bn_m1, bf_m1), (bn_p1, bf_p1), (bn_p2, bf_p2)],
        [place(dz, dx) for dx in (0, -1, 1, 2) for dz in near + far],
    )

    def by_tile(array):
        mine = of_core(array, array.ndim - 1, core)
        tiled = mine.reshape(mine.shape[:-1] + (4, LANES))
        return jnp.concatenate([tiled, tiled], axis=-2)

    rates = by_tile(decay_rates)
    gain = by_tile(residues) * jnp.sqrt(-jnp.expm1(-2.0 * rates))
    decay = jnp.exp(-rates)
    halves = (jnp.arange(8) // 4).astype(f32)[None, :, None]
    reach = jnp.exp(-rates * (halves * float(rows)))
    chip_decay = jnp.exp(-rates[:, :4] * float(2 * rows))
    taps = by_tile(short_taps)

    gated, end_first, end = gate(rows, weight0, projected_a, projected_b, taps, decay, reach)

    sent = jnp.broadcast_to(end.reshape(1, MODES, half).astype(bf16), (nz * nx, MODES, half))
    ends = lax.all_to_all(sent, ("z", "x"), 0, 0).reshape(nz * nx, MODES, 4, LANES)
    projected0 = project_all(core1, normed, weight0, half)
    spot = jnp.stack([core, z * nx + x])
    mine, to_swap = convolve(
        rows,
        spot,
        feature(rows, projected0, taps),
        gated,
        end_first,
        ends,
        decay,
        gain,
        reach,
        chip_decay,
        by_tile(bypass),
    )
    theirs = shift(to_swap, "core", 1)

    def blocks(dy):
        at = ((chan + dy) % ny) * 2
        return [at, at + 1]

    far0, far1 = output(core, blocks(2), mine, theirs, out_weight, [bf16, bf16])
    next0, next1, prev0, prev1 = output(
        core, blocks(1) + blocks(-1), mine, theirs, out_weight, [f32, bf16, bf16, f32]
    )
    own0, own1 = output(core, blocks(0), mine, theirs, out_weight, [f32, f32])
    via0, via1 = shift(far0, "chan", 1), shift(far1, "chan", -1)
    from_prev1, from_next0 = shift(next1, "chan", 1), shift(prev0, "chan", -1)
    from_prev0 = shift(add(next0, via0), "chan", 1)
    from_next1 = shift(add(prev1, via1), "chan", -1)
    return finish(own0, own1, from_prev0, from_prev1, from_next0, from_next1)


def solution(mesh):
    grid = mesh.devices.reshape(8, 4, 2, 4)
    fine = Mesh(grid, ("z", "x", "core", "chan"))
    seq = ("z", "x", "core")
    in_specs = (
        P(seq, None),
        P(),
        P(seq, None, "chan"),
        P(None, None, "chan"),
        P(None, "chan"),
        P(None, "chan"),
        P("chan"),
        P("chan", None),
    )
    return jax.shard_map(
        on_device, mesh=fine, in_specs=in_specs, out_specs=P(seq, "chan"), check_vma=False
    )
```
